512 devices in a mesh: row: 16 (over y, x), col: 32 (over z, core).
Axes of the slice: x: 4, y: 4, z: 16, core: 2. Of those that a mesh axis runs over, the one named last changes fastest.
Arguments:
- points: bfloat16 [262144, 256], P(('col', 'row')), may hold values from -6 to 6
- weights: bfloat16 [262144, 128], P(('col', 'row')), may hold values from -6 to 6
- near_blocks: int32 [2048, 16], P(('col', 'row')), may hold values from 0 to 2047, as said below
- proxies: bfloat16 [64, 256], replicated, may hold values from -6 to 6
Outputs:
- near_product: bfloat16 [262144, 128], P(('col', 'row'))
- factors: float32 [32768, 192], P(('col', 'row'))
The draws below stay inside these ranges and needn't reach their ends.
Inputs may be any that keep to these rules, and one draw needn't show every extreme that they name: near_blocks[j, 0] = j; every entry of row j lies in the column group of j, that is in the same run of 64 blocks; entries may repeat.
All inputs are finite; a program needn't handle non-finite values.
Results may differ from the reference program's by a relative error of at most 0.01.
Values may be sent and summed in bfloat16 or wider, within the bound.
No kernel may reach another device: no remote copies, remote signals or barrier semaphores. Data moves between devices by JAX's collectives and lax.ppermute only.
A program may use at most 64 MiB of HBM per device.

```python
import jax
import jax.numpy as jnp
import numpy as np
from jax import lax

DIM = 256
RANK = 64
BLK = 128
NV = 128
NNZ = 16
NB_DEV = 4
GROUP_BLOCKS = 64
BLOCKS = 2048
NPTS = 262144


def draw_near_blocks(key, part):
    key = jax.random.fold_in(key, 5)
    source = jnp.arange(BLOCKS, dtype=jnp.int32)
    base = source // GROUP_BLOCKS * GROUP_BLOCKS
    offsets = jax.random.randint(key, (BLOCKS, NNZ), 0, GROUP_BLOCKS, dtype=jnp.int32)
    result = base[:, None] + offsets
    return result.at[:, 0].set(source)


def block_levels(key, dims, split, least, high):
    def one(axis_at, parts):
        steps = jax.random.uniform(jax.random.fold_in(jax.random.fold_in(key, 6), axis_at), (parts,), jnp.float32, least / len(split), high / len(split))
        return jnp.repeat(jnp.exp(steps), dims[axis_at] // parts).reshape((-1,) + (1,) * (len(dims) - axis_at - 1))

    level = one(*split[0])
    for cut in split[1:]:
        level = level * one(*cut)
    return level


def scatter_about(rng, dims, deviation, limit, cuts=(), kind=jnp.bfloat16):
    array = jax.random.normal(rng, dims, jnp.float32) * deviation
    if len(cuts) > 0:
        array = block_levels(rng, dims, cuts, -0.22, 0.18) * array
    return jnp.clip(array, min=-limit, max=limit).astype(kind)


def setup_inputs(seed: int = 0) -> dict:
    keys = jax.random.split(jax.random.key(seed), 5)
    return {
        "points": scatter_about(keys[0], (NPTS, DIM), 1.0, 6.0, ((0, 512),)),
        "weights": scatter_about(keys[1], (NPTS, NV), 1.0, 6.0, ((0, 512),)),
        "near_blocks": draw_near_blocks(jax.random.fold_in(keys[4], 71), 0),
        "proxies": scatter_about(keys[3], (RANK, DIM), 1.0, 6.0),
    }


def kern_tile(left, right):
    cross = jnp.dot(left.astype(jnp.float32), right.T.astype(jnp.float32), preferred_element_type=jnp.float32)
    lnorm = jnp.sum(left.astype(jnp.float32) ** 2, axis=-1)
    rnorm = jnp.sum(right.astype(jnp.float32) ** 2, axis=-1)
    return jnp.exp(-(lnorm[:, None] + rnorm[None, :] - 2.0 * cross) * (2.0 / DIM))

def level_merge(lower_own, lower_other):
    hp = lax.Precision.HIGHEST
    gram = jnp.dot(lower_own, lower_own.T, precision=hp) + jnp.dot(lower_other, lower_other.T, precision=hp)
    merged = jnp.linalg.cholesky(gram)
    transfer = lax.linalg.triangular_solve(merged, lower_own, left_side=True, lower=True).T
    return (merged, transfer)

def leaf_factor(leaf_points, proxies):
    far = kern_tile(leaf_points, proxies)
    gram = jnp.dot(far.T, far, precision=lax.Precision.HIGHEST)
    return jnp.linalg.cholesky(gram)

def group_near(args):
    group_points, group_weights, group_near_ids, base = args
    tblocks = group_points.reshape(GROUP_BLOCKS, BLK, DIM)
    wblocks = group_weights.reshape(GROUP_BLOCKS, BLK, NV)
    local_ids = group_near_ids - base

    def one_source(partial_value, index):
        ids = local_ids[index]
        targets = tblocks[ids].reshape(NNZ * BLK, DIM)
        tile = kern_tile(targets, tblocks[index]).astype(jnp.bfloat16)
        contrib = jnp.dot(tile.astype(jnp.float32), wblocks[index].astype(jnp.float32), preferred_element_type=jnp.float32)
        return (partial_value.at[ids].add(contrib.reshape(NNZ, BLK, NV)), None)
    zeros = jnp.zeros((GROUP_BLOCKS, BLK, NV), jnp.float32)
    partial_value, unused = lax.scan(one_source, zeros, jnp.arange(GROUP_BLOCKS, dtype=jnp.int32))
    return partial_value.reshape(GROUP_BLOCKS * BLK, NV)

def reference(points, weights, near_blocks, proxies):
    n_col = BLOCKS // GROUP_BLOCKS
    n_row = GROUP_BLOCKS // NB_DEV
    group_points = points.reshape(n_col, GROUP_BLOCKS * BLK, DIM)
    group_weights = weights.reshape(n_col, GROUP_BLOCKS * BLK, NV)
    group_ids = near_blocks.reshape(n_col, GROUP_BLOCKS, NNZ)
    bases = (jnp.arange(n_col, dtype=jnp.int32) * GROUP_BLOCKS).astype(jnp.int32)
    near = lax.map(group_near, (group_points, group_weights, group_ids, bases))
    near_product = near.reshape(NPTS, NV).astype(jnp.bfloat16)
    leaves = points.reshape(n_col * n_row, NB_DEV * BLK, DIM)
    lower0 = lax.map(lambda leaf: leaf_factor(leaf, proxies), leaves).reshape(n_col, n_row, RANK, RANK)
    cols = np.arange(n_col)
    lower1, trans1 = jax.vmap(jax.vmap(level_merge))(lower0, lower0[cols ^ 1])
    lower2, trans2 = jax.vmap(jax.vmap(level_merge))(lower1, lower1[cols ^ 2])
    factors = jnp.concatenate([trans1, trans2, jnp.swapaxes(lower2, -1, -2)], axis=-1)
    return (near_product, factors.reshape(n_col * n_row * RANK, 3 * RANK))
```

```python
import functools

import jax
import jax.numpy as jnp
import numpy as np
from jax import lax
from jax.experimental import pallas as pl
from jax.experimental.pallas import tpu as pltpu
from jax.sharding import PartitionSpec as P

DIM = 256
RANK = 64
BLK = 128
NV = 128
UNIT = 512
NB = 4
SIDE = 4
EXTRA = 16
ROWS = UNIT + EXTRA
GROUP = 64
LOG2E = 1.4426950408889634
MASKS = (0, 1, 3, 2)
NT = (((1,), (1,)), ((), ()))
HIGH = lax.Precision.HIGHEST
VMEM = 24 * 1024 * 1024


def dot_nt(a, b, precision=None):
    return lax.dot_general(a, b, NT, precision=precision, preferred_element_type=jnp.float32)


def split2(x):
    hi = x.astype(jnp.bfloat16)
    return hi, (x - hi.astype(jnp.float32)).astype(jnp.bfloat16)


def prepare_kernel(points, weights, near, proxies, send, gram, scale):
    p = points[...]
    send[:UNIT, :DIM] = p
    send[:UNIT, DIM:] = weights[...]
    f = p.astype(jnp.float32)
    hi, lo = split2(f * f)
    ones = jnp.ones((8, DIM), jnp.bfloat16)
    norm = dot_nt(ones, hi) + dot_nt(ones, lo)
    tall = jnp.ones((DIM, NV), jnp.bfloat16)
    column = jnp.dot(hi, tall, preferred_element_type=jnp.float32) + jnp.dot(
        lo, tall, preferred_element_type=jnp.float32
    )
    scale[...] = jnp.exp(column * (-2.0 / DIM))
    ids = near[...] & (GROUP - 1)
    lanes = lax.broadcasted_iota(jnp.int32, (NB, BLK), 1)
    counts = jnp.zeros((NB, BLK), jnp.float32)
    for t in range(near.shape[1]):
        counts = counts + jnp.where(ids[:, t : t + 1] == lanes, 1.0, 0.0)
    rows = jnp.concatenate([norm[0:1, b * BLK : (b + 1) * BLK] for b in range(NB)], axis=0)
    first = rows.astype(jnp.bfloat16).astype(jnp.float32)
    second = (rows - first).astype(jnp.bfloat16).astype(jnp.float32)
    third = rows - first - second
    extra = jnp.concatenate([counts, first, second, third], axis=0)
    send[UNIT:, :BLK] = extra.astype(jnp.bfloat16)
    send[UNIT:, BLK:] = jnp.zeros((EXTRA, DIM + NV - BLK), jnp.bfloat16)
    q = proxies[...]
    qf = q.astype(jnp.float32)
    qnorm = jnp.sum(qf * qf, axis=1, keepdims=True)
    cross = dot_nt(q, p)
    far = jnp.exp((qnorm + norm[0:1, :] - 2.0 * cross) * (-2.0 / DIM))
    gram[...] = dot_nt(far, far, HIGH)


def factor_kernel(g0, s1, s2, out):
    zeros = jnp.zeros((RANK, RANK), jnp.float32)
    rows = lax.broadcasted_iota(jnp.int32, (RANK, 2 * RANK), 0)
    lanes = lax.broadcasted_iota(jnp.int32, (RANK, 2 * RANK), 1)
    eye = jnp.where(rows == lanes - RANK, 1.0, 0.0)
    gram0 = g0[...]
    gram1 = gram0 + s1[...]
    gram2 = gram1 + s2[...]
    work = []
    for g in (gram0, gram1, gram2):
        full = jnp.concatenate([g, zeros], axis=1) + eye
        work.append([full[8 * b : 8 * b + 8, :] for b in range(RANK // 8)])
    sub = lax.broadcasted_iota(jnp.int32, (8, 2 * RANK), 0)
    lane = lax.broadcasted_iota(jnp.int32, (8, 2 * RANK), 1)
    for k in range(RANK - 1):
        b0, s0 = divmod(k, 8)
        for m in range(3):
            w = work[m]
            row = w[b0][s0 : s0 + 1, :]
            row = row * (-1.0 / row[:, k : k + 1])
            for b in range(b0, RANK // 8):
                if b == b0:
                    if s0 == 7:
                        continue
                    col = jnp.where(sub > s0, w[b][:, k : k + 1], 0.0)
                else:
                    col = w[b][:, k : k + 1]
                w[b] = w[b] + col * row
    uppers, inverses = [], []
    for m in range(3):
        done = []
        for b in range(RANK // 8):
            w = work[m][b]
            diag = jnp.sum(jnp.where(lane == sub + 8 * b, w, 0.0), axis=1, keepdims=True)
            w = w * lax.rsqrt(diag)
            done.append(jnp.where((lane >= RANK) | (lane >= sub + 8 * b), w, 0.0))
        full = jnp.concatenate(done, axis=0)
        uppers.append(full[:, :RANK])
        inverses.append(full[:, RANK:])
    out[:, 0:RANK] = dot_nt(uppers[0], inverses[1], HIGH)
    out[:, RANK : 2 * RANK] = dot_nt(uppers[1], inverses[2], HIGH)
    out[:, 2 * RANK :] = uppers[2]


def near_kernel(ids, t01, t23, s01, s23, own, out1, out2, out3, bias):
    def target(k):
        return (t01, t23)[k // 2][(k % 2) * UNIT : (k % 2 + 1) * UNIT, :]

    def source(k, lo, hi, first, last):
        base = (k % 2) * ROWS
        return (s01, s23)[k // 2][base + lo : base + hi, first:last]

    rows = lax.broadcasted_iota(jnp.int32, (4 * NB, BLK), 0)
    lanes = lax.broadcasted_iota(jnp.int32, (4 * NB, BLK), 1)
    wanted = jnp.zeros((4 * NB, BLK), jnp.int32)
    for k in range(4):
        wanted = jnp.where(rows // NB == k, ids[k] * NB + rows % NB, wanted)
    pick = jnp.where(wanted == lanes, 1.0, 0.0).astype(jnp.bfloat16)
    for k in range(4):
        extra = source(k, UNIT, ROWS, 0, BLK)
        count = dot_nt(pick, extra)
        level = jnp.where(count > 0.5, jnp.log2(jnp.maximum(count, 1.0)), -1e30)
        parts = extra.astype(jnp.float32)
        for b in range(NB):
            norm = parts[NB + b : NB + b + 1] + parts[2 * NB + b : 2 * NB + b + 1] + parts[3 * NB + b : 3 * NB + b + 1]
            bias[:, k * UNIT + b * BLK : k * UNIT + (b + 1) * BLK] = (
                level[:, b : b + 1] - norm * (2.0 * LOG2E / DIM)
            )
    for t, out in ((3, out3), (2, out2), (1, out1), (0, own)):
        left = target(t)
        total = None
        for k in range(4):
            cross = dot_nt(left, source(k, 0, UNIT, 0, DIM))
            tiles = []
            for b in range(NB):
                i = t * NB + b
                row = bias[i : i + 1, k * UNIT : (k + 1) * UNIT]
                tiles.append(
                    jnp.exp2(cross[b * BLK : (b + 1) * BLK, :] * (4.0 * LOG2E / DIM) + row).astype(jnp.bfloat16)
                )
            tile = jnp.concatenate(tiles, axis=0)
            part = jnp.dot(tile, source(k, 0, UNIT, DIM, DIM + NV), preferred_element_type=jnp.float32)
            total = part if total is None else total + part
        out[...] = total.astype(out.dtype)


def finish_kernel(own, r1, r2, r3, scale, out):
    total = (
        own[...] + r1[...].astype(jnp.float32) + r2[...].astype(jnp.float32) + r3[...].astype(jnp.float32)
    )
    out[...] = (total * scale[...]).astype(jnp.bfloat16)


def call(kernel, shapes, *args, scratch=(), scalars=0, flops=0, nbytes=0):
    return pl.pallas_call(
        kernel,
        out_shape=shapes,
        in_specs=[pl.BlockSpec(memory_space=pltpu.SMEM)] * scalars
        + [pl.BlockSpec(memory_space=pltpu.VMEM)] * (len(args) - scalars),
        out_specs=jax.tree.map(lambda _: pl.BlockSpec(memory_space=pltpu.VMEM), shapes),
        scratch_shapes=list(scratch),
        compiler_params=pltpu.CompilerParams(vmem_limit_bytes=VMEM),
        cost_estimate=pl.CostEstimate(flops=flops, bytes_accessed=nbytes, transcendentals=0),
    )(*args)


def exchange(value, mask, first):
    n_col = lax.axis_size("col")
    pairs = []
    for y in range(SIDE):
        for x in range(SIDE):
            for c in range(n_col):
                along_x = c % 2 == first
                other = y * SIDE + (x ^ mask) if along_x else (y ^ mask) * SIDE + x
                pairs.append(((y * SIDE + x) * n_col + c, other * n_col + c))
    return lax.ppermute(value, ("row", "col"), pairs)


def partner(value, mask):
    return lax.ppermute(value, "col", [(c, c ^ mask) for c in range(lax.axis_size("col"))])


def on_device(points, weights, near_blocks, proxies):
    f32, bf16 = jnp.float32, jnp.bfloat16
    shape = jax.ShapeDtypeStruct
    send, gram, scale = call(
        prepare_kernel,
        (shape((ROWS, DIM + NV), bf16), shape((RANK, RANK), f32), shape((UNIT, NV), f32)),
        points,
        weights,
        near_blocks,
        proxies,
    )
    s1 = exchange(send, 1, 1)
    t1 = exchange(points, 3, 0)
    g1 = partner(gram, 1)
    s01 = jnp.concatenate([send, s1], axis=0)
    t01 = jnp.concatenate([points, t1], axis=0)
    s23 = exchange(s01, 3, 1)
    t23 = exchange(t01, 1, 0)
    g2 = partner(gram + g1, 2)
    factors = call(factor_kernel, shape((RANK, 3 * RANK), f32), gram, g1, g2)
    row = lax.axis_index("row")
    even = lax.axis_index("col") % 2 == 0
    ids = jnp.stack([jnp.where(even, row ^ m, row ^ (m * SIDE)) for m in (0, 3, 1, 2)]).astype(jnp.int32)
    own, p1, p2, p3 = call(
        near_kernel,
        (shape((UNIT, NV), f32),) + (shape((UNIT, NV), bf16),) * 3,
        ids,
        t01,
        t23,
        s01,
        s23,
        scratch=[pltpu.VMEM((4 * NB, 4 * UNIT), f32)],
        scalars=1,
    )
    r3 = exchange(p3, 2, 0)
    r2 = exchange(p2, 1, 0)
    r1 = exchange(p1, 3, 0)
    near_product = call(finish_kernel, shape((UNIT, NV), bf16), own, r1, r2, r3, scale)
    return (near_product, factors)


def solution(mesh):
    placed = (P(("col", "row"), None), P(("col", "row"), None), P(("col", "row"), None), P())
    return jax.shard_map(
        on_device,
        mesh=mesh,
        in_specs=placed,
        out_specs=(P(("col", "row"), None), P(("col", "row"), None)),
        check_vma=False,
    )
```

```python
import functools

import jax
import jax.numpy as jnp
import numpy as np
from jax import lax
from jax.experimental import pallas as pl
from jax.experimental.pallas import tpu as pltpu
from jax.sharding import PartitionSpec as P

DIM = 256
RANK = 64
BLK = 128
NV = 128
UNIT = 512
NB = 4
SIDE = 4
EXTRA = 16
ROWS = UNIT + EXTRA
GROUP = 64
LOG2E = 1.4426950408889634
LINE = 4
PANEL = 4
NT = (((1,), (1,)), ((), ()))
HIGH = lax.Precision.HIGHEST
VMEM = 24 * 1024 * 1024
SEND_VMEM = 62 * 1024 * 1024


def dot_nt(a, b, precision=None):
    return lax.dot_general(a, b, NT, precision=precision, preferred_element_type=jnp.float32)


def split2(x):
    hi = x.astype(jnp.bfloat16)
    return hi, (x - hi.astype(jnp.float32)).astype(jnp.bfloat16)


def row_norms(squares):
    hi, lo = squares
    ones = jnp.ones((8, DIM), jnp.bfloat16)
    return dot_nt(ones, hi) + dot_nt(ones, lo)


def send_kernel(points, weights, near, send, ids, sems):
    copies = [
        pltpu.make_async_copy(points, send.at[pl.ds(0, UNIT), pl.ds(0, DIM)], sems.at[0]),
        pltpu.make_async_copy(near, ids, sems.at[1]),
        pltpu.make_async_copy(weights, send.at[pl.ds(0, UNIT), pl.ds(DIM, NV)], sems.at[2]),
    ]
    for copy in copies:
        copy.start()
    send[UNIT:, BLK:] = jnp.zeros((EXTRA, DIM + NV - BLK), jnp.bfloat16)
    copies[1].wait()
    local = ids[...] & (GROUP - 1)
    lanes = lax.broadcasted_iota(jnp.int32, (NB, BLK), 1)
    counts = jnp.zeros((NB, BLK), jnp.float32)
    for t in range(near.shape[1]):
        counts = counts + jnp.where(local[:, t : t + 1] == lanes, 1.0, 0.0)
    copies[0].wait()
    f = send[:UNIT, :DIM].astype(jnp.float32)
    norm = row_norms(split2(f * f))
    rows = jnp.concatenate([norm[0:1, b * BLK : (b + 1) * BLK] for b in range(NB)], axis=0)
    first = rows.astype(jnp.bfloat16).astype(jnp.float32)
    second = (rows - first).astype(jnp.bfloat16).astype(jnp.float32)
    third = rows - first - second
    extra = jnp.concatenate([counts, first, second, third], axis=0)
    send[UNIT:, :BLK] = extra.astype(jnp.bfloat16)
    copies[2].wait()


def gram_kernel(send, proxies, gram, scale):
    p = send[:UNIT, :DIM]
    f = p.astype(jnp.float32)
    squares = split2(f * f)
    tall = jnp.ones((DIM, NV), jnp.bfloat16)
    column = jnp.dot(squares[0], tall, preferred_element_type=jnp.float32) + jnp.dot(
        squares[1], tall, preferred_element_type=jnp.float32
    )
    scale[...] = jnp.exp(column * (-2.0 / DIM))
    q = proxies[...]
    qf = q.astype(jnp.float32)
    qnorm = jnp.sum(qf * qf, axis=1, keepdims=True)
    far = jnp.exp((qnorm + row_norms(squares)[0:1, :] - 2.0 * dot_nt(q, p)) * (-2.0 / DIM))
    gram[...] = dot_nt(far, far, HIGH)


def factor_kernel(g0, s1, s2, out):
    zeros = jnp.zeros((RANK, RANK), jnp.float32)
    rows = lax.broadcasted_iota(jnp.int32, (RANK, 2 * RANK), 0)
    lanes = lax.broadcasted_iota(jnp.int32, (RANK, 2 * RANK), 1)
    eye = jnp.where(rows == lanes - RANK, 1.0, 0.0)
    gram0 = g0[...]
    gram1 = gram0 + s1[...]
    gram2 = gram1 + s2[...]
    work = []
    for g in (gram0, gram1, gram2):
        full = jnp.concatenate([g, zeros], axis=1) + eye
        work.append([full[8 * b : 8 * b + 8, :] for b in range(RANK // 8)])
    sub = lax.broadcasted_iota(jnp.int32, (8, 2 * RANK), 0)
    lane = lax.broadcasted_iota(jnp.int32, (8, 2 * RANK), 1)
    for k0 in range(0, RANK, PANEL):
        b0 = k0 // 8
        cols = [
            [
                {b: jnp.broadcast_to(w[b][:, k : k + 1], (8, 2 * RANK)) for b in range(b0, RANK // 8)}
                for k in range(k0, k0 + PANEL)
            ]
            for w in work
        ]
        for j in range(PANEL):
            s0 = (k0 + j) % 8
            for w, c in zip(work, cols):
                inverse = -1.0 / c[j][b0][s0 : s0 + 1, :]
                row = w[b0][s0 : s0 + 1, :] * inverse
                later = [c[i][b0][s0 : s0 + 1, :] * inverse for i in range(j + 1, PANEL)]
                for b in range(b0, RANK // 8):
                    col = c[j][b]
                    if b == b0:
                        if s0 == 7:
                            continue
                        col = jnp.where(sub > s0, col, 0.0)
                    w[b] = w[b] + col * row
                    for i, entry in enumerate(later, j + 1):
                        c[i][b] = c[i][b] + col * entry
    uppers, inverses = [], []
    for m in range(3):
        done = []
        for b in range(RANK // 8):
            w = work[m][b]
            diag = jnp.sum(jnp.where(lane == sub + 8 * b, w, 0.0), axis=1, keepdims=True)
            w = w * lax.rsqrt(diag)
            done.append(jnp.where((lane >= RANK) | (lane >= sub + 8 * b), w, 0.0))
        full = jnp.concatenate(done, axis=0)
        uppers.append(full[:, :RANK])
        inverses.append(full[:, RANK:])
    out[:, 0:RANK] = dot_nt(uppers[0], inverses[1], HIGH)
    out[:, RANK : 2 * RANK] = dot_nt(uppers[1], inverses[2], HIGH)
    out[:, 2 * RANK :] = uppers[2]


def bias_rows(ids, sources, bias):
    rows = lax.broadcasted_iota(jnp.int32, (LINE * NB, BLK), 0)
    lanes = lax.broadcasted_iota(jnp.int32, (LINE * NB, BLK), 1)
    wanted = jnp.zeros((LINE * NB, BLK), jnp.int32)
    for k in range(LINE):
        wanted = jnp.where(rows // NB == k, ids[k] * NB + rows % NB, wanted)
    pick = jnp.where(wanted == lanes, 1.0, 0.0).astype(jnp.bfloat16)
    for k, source in enumerate(sources):
        extra = source[UNIT:ROWS, :BLK]
        count = dot_nt(pick, extra)
        level = jnp.where(count > 0.5, jnp.log2(jnp.maximum(count, 1.0)), -1e30)
        parts = extra.astype(jnp.float32)
        for b in range(NB):
            norm = parts[NB + b : NB + b + 1] + parts[2 * NB + b : 2 * NB + b + 1] + parts[3 * NB + b : 3 * NB + b + 1]
            bias[:, k * UNIT + b * BLK : k * UNIT + (b + 1) * BLK] = (
                level[:, b : b + 1] - norm * (2.0 * LOG2E / DIM)
            )


def near_sum(left, t, sources, bias, total=None):
    for k, source in enumerate(sources):
        cross = dot_nt(left, source[:UNIT, :DIM])
        tiles = []
        for b in range(NB):
            i = t * NB + b
            row = bias[i : i + 1, k * UNIT : (k + 1) * UNIT]
            tiles.append(
                jnp.exp2(cross[b * BLK : (b + 1) * BLK, :] * (4.0 * LOG2E / DIM) + row).astype(jnp.bfloat16)
            )
        tile = jnp.concatenate(tiles, axis=0)
        part = jnp.dot(tile, source[:UNIT, DIM:], preferred_element_type=jnp.float32)
        total = part if total is None else total + part
    return total


def near_first_kernel(ids, s0, s1, t1, own, other, bias):
    bias_rows(ids, (s0, s1), bias)
    own[...] = near_sum(s0[:UNIT, :DIM], 0, (s0, s1), bias)
    other[...] = near_sum(t1[...], 1, (s0, s1), bias)


def near_out_kernel(ids, s0, s1, s2, s3, t1, t23, other, bias01, out, bias):
    bias_rows(ids, (s2, s3), bias)
    total = near_sum(t23[UNIT:, :], 3, (s0, s1), bias01)
    out[UNIT:, :] = near_sum(t23[UNIT:, :], 3, (s2, s3), bias, total).astype(jnp.bfloat16)
    out[:UNIT, :] = near_sum(t1[...], 1, (s2, s3), bias, other[...]).astype(jnp.bfloat16)


def near_in_kernel(s0, s1, s2, s3, t23, own, bias01, bias, own_out, out):
    total = near_sum(t23[:UNIT, :], 2, (s0, s1), bias01)
    out[...] = near_sum(t23[:UNIT, :], 2, (s2, s3), bias, total)
    own_out[...] = near_sum(s0[:UNIT, :DIM], 0, (s2, s3), bias, own[...])


def relay_kernel(mine, received, out):
    out[...] = (mine[...] + received[UNIT:, :].astype(jnp.float32)).astype(jnp.bfloat16)


def finish_kernel(own, first, second, scale, out):
    total = own[...] + first[:UNIT, :].astype(jnp.float32) + second[...].astype(jnp.float32)
    out[...] = (total * scale[...]).astype(jnp.bfloat16)


def call(kernel, shapes, *args, scratch=(), scalars=0, space=pltpu.VMEM, vmem=VMEM):
    return pl.pallas_call(
        kernel,
        out_shape=shapes,
        in_specs=[pl.BlockSpec(memory_space=pltpu.SMEM)] * scalars
        + [pl.BlockSpec(memory_space=space)] * (len(args) - scalars),
        out_specs=jax.tree.map(lambda _: pl.BlockSpec(memory_space=pltpu.VMEM), shapes),
        scratch_shapes=list(scratch),
        compiler_params=pltpu.CompilerParams(vmem_limit_bytes=vmem),
    )(*args)


def exchange(value, mask, first):
    n_col = lax.axis_size("col")
    pairs = []
    for y in range(SIDE):
        for x in range(SIDE):
            for c in range(n_col):
                along_x = c % 2 == first
                other = y * SIDE + (x ^ mask) if along_x else (y ^ mask) * SIDE + x
                pairs.append(((y * SIDE + x) * n_col + c, other * n_col + c))
    return lax.ppermute(value, ("row", "col"), pairs)


def partner(value, mask):
    return lax.ppermute(value, "col", [(c, c ^ mask) for c in range(lax.axis_size("col"))])


def on_device(points, weights, near_blocks, proxies):
    f32, bf16 = jnp.float32, jnp.bfloat16
    shape = jax.ShapeDtypeStruct
    t1 = exchange(points, 1, 0)
    send = call(
        send_kernel,
        shape((ROWS, DIM + NV), bf16),
        points,
        weights,
        near_blocks,
        scratch=[pltpu.VMEM(near_blocks.shape, jnp.int32), pltpu.SemaphoreType.DMA((3,))],
        space=pltpu.HBM,
        vmem=SEND_VMEM,
    )
    s1 = exchange(send, 3, 1)
    s2 = exchange(send, 1, 1)
    t23 = exchange(jnp.concatenate([points, t1], axis=0), 3, 0)
    proxies, t1 = lax.optimization_barrier((proxies, t1))
    gram, scale = call(gram_kernel, (shape((RANK, RANK), f32), shape((UNIT, NV), f32)), send, proxies)
    s3 = exchange(s1, 1, 1)
    gram, s1 = lax.optimization_barrier((gram, s1))
    g1 = partner(gram, 1)
    row = lax.axis_index("row")
    odd = lax.axis_index("col") % 2
    ids = jnp.stack([jnp.where(odd == 1, row ^ (m * SIDE), row ^ m) for m in (0, 1, 3, 2)]).astype(jnp.int32)
    half = shape((LINE * NB, 2 * UNIT), f32)
    unit = shape((UNIT, NV), f32)
    own, other, bias01 = call(near_first_kernel, (unit, unit, half), ids, send, s1, t1, scalars=1)
    level1, later_ids = lax.optimization_barrier((gram + g1, ids))
    g2 = partner(level1, 2)
    out, bias23 = call(
        near_out_kernel,
        (shape((2 * UNIT, NV), bf16), half),
        later_ids,
        send,
        s1,
        s2,
        s3,
        t1,
        t23,
        other,
        bias01,
        scalars=1,
    )
    r1 = exchange(out, 1, 0)
    own, mine = call(near_in_kernel, (unit, unit), send, s1, s2, s3, t23, own, bias01, bias23)
    mine, g2 = lax.optimization_barrier((mine, g2))
    relayed = call(relay_kernel, shape((UNIT, NV), bf16), mine, r1)
    r2 = exchange(relayed, 3, 0)
    gram, own = lax.optimization_barrier((gram, own))
    factors = call(factor_kernel, shape((RANK, 3 * RANK), f32), gram, g1, g2)
    near_product = call(finish_kernel, shape((UNIT, NV), bf16), own, r1, r2, scale)
    return (near_product, factors)


def solution(mesh):
    placed = (P(("col", "row"), None), P(("col", "row"), None), P(("col", "row"), None), P())
    return jax.shard_map(
        on_device,
        mesh=mesh,
        in_specs=placed,
        out_specs=(P(("col", "row"), None), P(("col", "row"), None)),
        check_vma=False,
    )
```

```python
import functools

import jax
import jax.numpy as jnp
import numpy as np
from jax import lax
from jax.experimental import pallas as pl
from jax.experimental.pallas import tpu as pltpu
from jax.sharding import PartitionSpec as P

DIM = 256
RANK = 64
BLK = 128
NV = 128
UNIT = 512
NB = 4
SIDE = 4
EXTRA = 16
ROWS = UNIT + EXTRA
GROUP = 64
LOG2E = 1.4426950408889634
LINE = 4
MASKS = (0, 1, 3, 2)
PANEL = 4
NT = (((1,), (1,)), ((), ()))
HIGH = lax.Precision.HIGHEST
VMEM = 24 * 1024 * 1024
SEND_VMEM = 62 * 1024 * 1024


def dot_nt(a, b, precision=None):
    return lax.dot_general(a, b, NT, precision=precision, preferred_element_type=jnp.float32)


def split2(x):
    hi = x.astype(jnp.bfloat16)
    return hi, (x - hi.astype(jnp.float32)).astype(jnp.bfloat16)


def row_norms(squares):
    hi, lo = squares
    ones = jnp.ones((8, DIM), jnp.bfloat16)
    return dot_nt(ones, hi) + dot_nt(ones, lo)


def send_kernel(points, weights, near, send, held, ids, sems):
    unit, left, right = pl.ds(0, UNIT), pl.ds(0, DIM), pl.ds(DIM, NV)
    arriving = [
        pltpu.make_async_copy(points, held.at[unit, left], sems.at[0]),
        pltpu.make_async_copy(near, ids, sems.at[1]),
        pltpu.make_async_copy(weights, held.at[unit, right], sems.at[2]),
    ]
    leaving = [
        pltpu.make_async_copy(held.at[unit, left], send.at[unit, left], sems.at[3]),
        pltpu.make_async_copy(held.at[unit, right], send.at[unit, right], sems.at[4]),
        pltpu.make_async_copy(held.at[pl.ds(UNIT, EXTRA), :], send.at[pl.ds(UNIT, EXTRA), :], sems.at[5]),
    ]
    for copy in arriving:
        copy.start()
    held[UNIT:, BLK:] = jnp.zeros((EXTRA, DIM + NV - BLK), jnp.bfloat16)
    arriving[1].wait()
    local = ids[...] & (GROUP - 1)
    lanes = lax.broadcasted_iota(jnp.int32, (NB, BLK), 1)
    counts = jnp.zeros((NB, BLK), jnp.float32)
    for t in range(near.shape[1]):
        counts = counts + jnp.where(local[:, t : t + 1] == lanes, 1.0, 0.0)
    arriving[0].wait()
    leaving[0].start()
    arriving[2].wait()
    leaving[1].start()
    f = held[:UNIT, :DIM].astype(jnp.float32)
    norm = row_norms(split2(f * f))
    rows = jnp.concatenate([norm[0:1, b * BLK : (b + 1) * BLK] for b in range(NB)], axis=0)
    first = rows.astype(jnp.bfloat16).astype(jnp.float32)
    second = (rows - first).astype(jnp.bfloat16).astype(jnp.float32)
    third = rows - first - second
    extra = jnp.concatenate([counts, first, second, third], axis=0)
    held[UNIT:, :BLK] = extra.astype(jnp.bfloat16)
    leaving[2].start()
    for copy in leaving:
        copy.wait()


def gram_kernel(points, proxies, gram, scale):
    p = points[...]
    f = p.astype(jnp.float32)
    squares = split2(f * f)
    tall = jnp.ones((DIM, NV), jnp.bfloat16)
    column = jnp.dot(squares[0], tall, preferred_element_type=jnp.float32) + jnp.dot(
        squares[1], tall, preferred_element_type=jnp.float32
    )
    scale[...] = jnp.exp(column * (-2.0 / DIM))
    q = proxies[...]
    qf = q.astype(jnp.float32)
    qnorm = jnp.sum(qf * qf, axis=1, keepdims=True)
    far = jnp.exp((qnorm + row_norms(squares)[0:1, :] - 2.0 * dot_nt(q, p)) * (-2.0 / DIM))
    gram[...] = dot_nt(far, far, HIGH)


def factor_kernel(g0, s1, s2, out):
    zeros = jnp.zeros((RANK, RANK), jnp.float32)
    rows = lax.broadcasted_iota(jnp.int32, (RANK, 2 * RANK), 0)
    lanes = lax.broadcasted_iota(jnp.int32, (RANK, 2 * RANK), 1)
    eye = jnp.where(rows == lanes - RANK, 1.0, 0.0)
    gram0 = g0[...]
    gram1 = gram0 + s1[...]
    gram2 = gram1 + s2[...]
    work = []
    for g in (gram0, gram1, gram2):
        full = jnp.concatenate([g, zeros], axis=1) + eye
        work.append([full[8 * b : 8 * b + 8, :] for b in range(RANK // 8)])
    sub = lax.broadcasted_iota(jnp.int32, (8, 2 * RANK), 0)
    lane = lax.broadcasted_iota(jnp.int32, (8, 2 * RANK), 1)
    for k0 in range(0, RANK, PANEL):
        b0 = k0 // 8
        cols = [
            [
                {b: jnp.broadcast_to(w[b][:, k : k + 1], (8, 2 * RANK)) for b in range(b0, RANK // 8)}
                for k in range(k0, k0 + PANEL)
            ]
            for w in work
        ]
        for j in range(PANEL):
            s0 = (k0 + j) % 8
            for w, c in zip(work, cols):
                inverse = -1.0 / c[j][b0][s0 : s0 + 1, :]
                row = w[b0][s0 : s0 + 1, :] * inverse
                later = [c[i][b0][s0 : s0 + 1, :] * inverse for i in range(j + 1, PANEL)]
                for b in range(b0, RANK // 8):
                    col = c[j][b]
                    if b == b0:
                        if s0 == 7:
                            continue
                        col = jnp.where(sub > s0, col, 0.0)
                    w[b] = w[b] + col * row
                    for i, entry in enumerate(later, j + 1):
                        c[i][b] = c[i][b] + col * entry
    uppers, inverses = [], []
    for m in range(3):
        done = []
        for b in range(RANK // 8):
            w = work[m][b]
            diag = jnp.sum(jnp.where(lane == sub + 8 * b, w, 0.0), axis=1, keepdims=True)
            w = w * lax.rsqrt(diag)
            done.append(jnp.where((lane >= RANK) | (lane >= sub + 8 * b), w, 0.0))
        full = jnp.concatenate(done, axis=0)
        uppers.append(full[:, :RANK])
        inverses.append(full[:, RANK:])
    out[:, 0:RANK] = dot_nt(uppers[0], inverses[1], HIGH)
    out[:, RANK : 2 * RANK] = dot_nt(uppers[1], inverses[2], HIGH)
    out[:, 2 * RANK :] = uppers[2]


def bias_rows(sources, bias):
    row, odd = lax.axis_index("row"), lax.axis_index("col") & 1
    rows = lax.broadcasted_iota(jnp.int32, (LINE * NB, BLK), 0)
    lanes = lax.broadcasted_iota(jnp.int32, (LINE * NB, BLK), 1)
    wanted = jnp.zeros((LINE * NB, BLK), jnp.int32)
    for k, mask in enumerate(MASKS):
        unit = row ^ (mask * (1 + (SIDE - 1) * odd))
        wanted = jnp.where(rows // NB == k, unit * NB + rows % NB, wanted)
    pick = jnp.where(wanted == lanes, 1.0, 0.0).astype(jnp.bfloat16)
    for k, source in enumerate(sources):
        extra = source[UNIT:ROWS, :BLK]
        count = dot_nt(pick, extra)
        level = jnp.where(count > 0.5, jnp.log2(jnp.maximum(count, 1.0)), -1e30)
        parts = extra.astype(jnp.float32)
        for b in range(NB):
            norm = parts[NB + b : NB + b + 1] + parts[2 * NB + b : 2 * NB + b + 1] + parts[3 * NB + b : 3 * NB + b + 1]
            bias[:, k * UNIT + b * BLK : k * UNIT + (b + 1) * BLK] = (
                level[:, b : b + 1] - norm * (2.0 * LOG2E / DIM)
            )


def near_sum(left, t, sources, bias, total=None):
    for k, source in enumerate(sources):
        cross = dot_nt(left, source[:UNIT, :DIM])
        tiles = []
        for b in range(NB):
            i = t * NB + b
            row = bias[i : i + 1, k * UNIT : (k + 1) * UNIT]
            tiles.append(
                jnp.exp2(cross[b * BLK : (b + 1) * BLK, :] * (4.0 * LOG2E / DIM) + row).astype(jnp.bfloat16)
            )
        tile = jnp.concatenate(tiles, axis=0)
        part = jnp.dot(tile, source[:UNIT, DIM:], preferred_element_type=jnp.float32)
        total = part if total is None else total + part
    return total


def near_first_kernel(s0, s1, t1, t23, own, *rest):
    others, bias = rest[:-1], rest[-1]
    bias_rows((s0, s1), bias)
    own[...] = near_sum(s0[:UNIT, :DIM], 0, (s0, s1), bias)
    lefts = (t1, t23.at[pl.ds(0, UNIT)], t23.at[pl.ds(UNIT, UNIT)])
    for t, (left, other) in enumerate(zip(lefts, others), 1):
        other[...] = near_sum(left[...], t, (s0, s1), bias)


def near_out_kernel(s2, s3, t1, t23, total1, total3, out, bias):
    bias_rows((s2, s3), bias)
    out[UNIT:, :] = near_sum(t23[UNIT:, :], 3, (s2, s3), bias, total3[...]).astype(jnp.bfloat16)
    out[:UNIT, :] = near_sum(t1[...], 1, (s2, s3), bias, total1[...]).astype(jnp.bfloat16)


def near_in_kernel(s0, s2, s3, t23, own, total2, bias, own_out, out):
    out[...] = near_sum(t23[:UNIT, :], 2, (s2, s3), bias, total2[...])
    own_out[...] = near_sum(s0[:UNIT, :DIM], 0, (s2, s3), bias, own[...])


def relay_kernel(mine, received, out):
    out[...] = (mine[...] + received[UNIT:, :].astype(jnp.float32)).astype(jnp.bfloat16)


def finish_kernel(own, first, second, scale, out):
    total = own[...] + first[:UNIT, :].astype(jnp.float32) + second[...].astype(jnp.float32)
    out[...] = (total * scale[...]).astype(jnp.bfloat16)


def call(kernel, shapes, *args, micros=1.0, scratch=(), space=pltpu.VMEM, vmem=VMEM):
    return pl.pallas_call(
        kernel,
        out_shape=shapes,
        in_specs=[pl.BlockSpec(memory_space=space)] * len(args),
        out_specs=jax.tree.map(lambda _: pl.BlockSpec(memory_space=space), shapes),
        scratch_shapes=list(scratch),
        compiler_params=pltpu.CompilerParams(vmem_limit_bytes=vmem),
        cost_estimate=pl.CostEstimate(flops=int(micros * 1e9), bytes_accessed=int(micros * 3e6), transcendentals=0),
    )(*args)


def exchange(value, mask, first):
    n_col = lax.axis_size("col")
    pairs = []
    for y in range(SIDE):
        for x in range(SIDE):
            for c in range(n_col):
                along_x = c % 2 == first
                other = y * SIDE + (x ^ mask) if along_x else (y ^ mask) * SIDE + x
                pairs.append(((y * SIDE + x) * n_col + c, other * n_col + c))
    return lax.ppermute(value, ("row", "col"), pairs)


def partner(value, mask):
    return lax.ppermute(value, "col", [(c, c ^ mask) for c in range(lax.axis_size("col"))])


def on_device(points, weights, near_blocks, proxies):
    f32, bf16 = jnp.float32, jnp.bfloat16
    shape = jax.ShapeDtypeStruct
    t1 = exchange(points, 1, 0)
    send = call(
        send_kernel,
        shape((ROWS, DIM + NV), bf16),
        points,
        weights,
        near_blocks,
        scratch=[
            pltpu.VMEM((ROWS, DIM + NV), bf16),
            pltpu.VMEM(near_blocks.shape, jnp.int32),
            pltpu.SemaphoreType.DMA((6,)),
        ],
        space=pltpu.HBM,
        vmem=SEND_VMEM,
    )
    s1 = exchange(send, 3, 1)
    s2 = exchange(send, 1, 1)
    t23 = exchange(jnp.concatenate([points, t1], axis=0), 3, 0)
    proxies, t1 = lax.optimization_barrier((proxies, t1))
    gram, scale = call(gram_kernel, (shape((RANK, RANK), f32), shape((UNIT, NV), f32)), points, proxies)
    s3 = exchange(s1, 1, 1)
    gram, s1 = lax.optimization_barrier((gram, s1))
    g1 = partner(gram, 1)
    half = shape((LINE * NB, 2 * UNIT), f32)
    unit = shape((UNIT, NV), f32)
    own, total1, total2, total3 = call(
        near_first_kernel,
        (unit,) * LINE,
        send,
        s1,
        t1,
        t23,
        scratch=[pltpu.VMEM(half.shape, f32)],
    )
    g1, total1 = lax.optimization_barrier((g1, total1))
    g2 = partner(gram + g1, 2)
    out, bias23 = call(
        near_out_kernel, (shape((2 * UNIT, NV), bf16), half), s2, s3, t1, t23, total1, total3
    )
    r1 = exchange(out, 1, 0)
    own, mine = call(near_in_kernel, (unit, unit), send, s2, s3, t23, own, total2, bias23)
    relayed = call(relay_kernel, shape((UNIT, NV), bf16), mine, r1)
    r2 = exchange(relayed, 3, 0)
    gram, own = lax.optimization_barrier((gram, own))
    factors = call(factor_kernel, shape((RANK, 3 * RANK), f32), gram, g1, g2, micros=3.4)
    near_product = call(finish_kernel, shape((UNIT, NV), bf16), own, r1, r2, scale)
    return (near_product, factors)


def solution(mesh):
    placed = (P(("col", "row"), None), P(("col", "row"), None), P(("col", "row"), None), P())
    return jax.shard_map(
        on_device,
        mesh=mesh,
        in_specs=placed,
        out_specs=(P(("col", "row"), None), P(("col", "row"), None)),
        check_vma=False,
    )
```

```python
import functools

import jax
import jax.numpy as jnp
import numpy as np
from jax import lax
from jax.experimental import pallas as pl
from jax.experimental.pallas import tpu as pltpu
from jax.sharding import PartitionSpec as P

DIM = 256
RANK = 64
BLK = 128
NV = 128
UNIT = 512
NB = 4
SIDE = 4
EXTRA = 16
ROWS = UNIT + EXTRA
GROUP = 64
LOG2E = 1.4426950408889634
LINE = 4
MASKS = (0, 1, 3, 2)
PANEL = 4
NT = (((1,), (1,)), ((), ()))
HIGH = lax.Precision.HIGHEST
VMEM = 24 * 1024 * 1024
SEND_VMEM = 62 * 1024 * 1024


def dot_nt(a, b, precision=None):
    return lax.dot_general(a, b, NT, precision=precision, preferred_element_type=jnp.float32)


def split2(x):
    hi = x.astype(jnp.bfloat16)
    return hi, (x - hi.astype(jnp.float32)).astype(jnp.bfloat16)


def row_norms(squares):
    hi, lo = squares
    ones = jnp.ones((8, DIM), jnp.bfloat16)
    return dot_nt(ones, hi) + dot_nt(ones, lo)


def send_kernel(points, weights, near, send, held, ids, sems):
    unit, left, right = pl.ds(0, UNIT), pl.ds(0, DIM), pl.ds(DIM, NV)
    arriving = [
        pltpu.make_async_copy(points, held.at[unit, left], sems.at[0]),
        pltpu.make_async_copy(near, ids, sems.at[1]),
        pltpu.make_async_copy(weights, held.at[unit, right], sems.at[2]),
    ]
    leaving = [
        pltpu.make_async_copy(held.at[unit, left], send.at[unit, left], sems.at[3]),
        pltpu.make_async_copy(held.at[unit, right], send.at[unit, right], sems.at[4]),
        pltpu.make_async_copy(held.at[pl.ds(UNIT, EXTRA), :], send.at[pl.ds(UNIT, EXTRA), :], sems.at[5]),
    ]
    for copy in arriving:
        copy.start()
    held[UNIT:, BLK:] = jnp.zeros((EXTRA, DIM + NV - BLK), jnp.bfloat16)
    arriving[1].wait()
    local = ids[...] & (GROUP - 1)
    lanes = lax.broadcasted_iota(jnp.int32, (NB, BLK), 1)
    counts = jnp.zeros((NB, BLK), jnp.float32)
    for t in range(near.shape[1]):
        counts = counts + jnp.where(local[:, t : t + 1] == lanes, 1.0, 0.0)
    arriving[0].wait()
    leaving[0].start()
    arriving[2].wait()
    leaving[1].start()
    f = held[:UNIT, :DIM].astype(jnp.float32)
    norm = row_norms(split2(f * f))
    rows = jnp.concatenate([norm[0:1, b * BLK : (b + 1) * BLK] for b in range(NB)], axis=0)
    first = rows.astype(jnp.bfloat16).astype(jnp.float32)
    second = (rows - first).astype(jnp.bfloat16).astype(jnp.float32)
    third = rows - first - second
    extra = jnp.concatenate([counts, first, second, third], axis=0)
    held[UNIT:, :BLK] = extra.astype(jnp.bfloat16)
    leaving[2].start()
    for copy in leaving:
        copy.wait()


def gram_kernel(points, proxies, gram, scale):
    p = points[...]
    f = p.astype(jnp.float32)
    squares = split2(f * f)
    tall = jnp.ones((DIM, NV), jnp.bfloat16)
    column = jnp.dot(squares[0], tall, preferred_element_type=jnp.float32) + jnp.dot(
        squares[1], tall, preferred_element_type=jnp.float32
    )
    scale[...] = jnp.exp(column * (-2.0 / DIM))
    q = proxies[...]
    qf = q.astype(jnp.float32)
    qnorm = jnp.sum(qf * qf, axis=1, keepdims=True)
    far = jnp.exp((qnorm + row_norms(squares)[0:1, :] - 2.0 * dot_nt(q, p)) * (-2.0 / DIM))
    gram[...] = dot_nt(far, far, HIGH)


def factor_kernel(g0, s1, s2, out):
    zeros = jnp.zeros((RANK, RANK), jnp.float32)
    rows = lax.broadcasted_iota(jnp.int32, (RANK, 2 * RANK), 0)
    lanes = lax.broadcasted_iota(jnp.int32, (RANK, 2 * RANK), 1)
    eye = jnp.where(rows == lanes - RANK, 1.0, 0.0)
    gram0 = g0[...]
    gram1 = gram0 + s1[...]
    gram2 = gram1 + s2[...]
    work = []
    for g in (gram0, gram1, gram2):
        full = jnp.concatenate([g, zeros], axis=1) + eye
        work.append([full[8 * b : 8 * b + 8, :] for b in range(RANK // 8)])
    sub = lax.broadcasted_iota(jnp.int32, (8, 2 * RANK), 0)
    lane = lax.broadcasted_iota(jnp.int32, (8, 2 * RANK), 1)
    for k0 in range(0, RANK, PANEL):
        b0 = k0 // 8
        cols = [
            [
                {b: jnp.broadcast_to(w[b][:, k : k + 1], (8, 2 * RANK)) for b in range(b0, RANK // 8)}
                for k in range(k0, k0 + PANEL)
            ]
            for w in work
        ]
        for j in range(PANEL):
            s0 = (k0 + j) % 8
            for w, c in zip(work, cols):
                inverse = -1.0 / c[j][b0][s0 : s0 + 1, :]
                row = w[b0][s0 : s0 + 1, :] * inverse
                later = [c[i][b0][s0 : s0 + 1, :] * inverse for i in range(j + 1, PANEL)]
                for b in range(b0, RANK // 8):
                    col = c[j][b]
                    if b == b0:
                        if s0 == 7:
                            continue
                        col = jnp.where(sub > s0, col, 0.0)
                    w[b] = w[b] + col * row
                    for i, entry in enumerate(later, j + 1):
                        c[i][b] = c[i][b] + col * entry
    uppers, inverses = [], []
    for m in range(3):
        done = []
        for b in range(RANK // 8):
            w = work[m][b]
            diag = jnp.sum(jnp.where(lane == sub + 8 * b, w, 0.0), axis=1, keepdims=True)
            w = w * lax.rsqrt(diag)
            done.append(jnp.where((lane >= RANK) | (lane >= sub + 8 * b), w, 0.0))
        full = jnp.concatenate(done, axis=0)
        uppers.append(full[:, :RANK])
        inverses.append(full[:, RANK:])
    out[:, 0:RANK] = dot_nt(uppers[0], inverses[1], HIGH)
    out[:, RANK : 2 * RANK] = dot_nt(uppers[1], inverses[2], HIGH)
    out[:, 2 * RANK :] = uppers[2]


def bias_rows(sources, bias):
    row, odd = lax.axis_index("row"), lax.axis_index("col") & 1
    rows = lax.broadcasted_iota(jnp.int32, (LINE * NB, BLK), 0)
    lanes = lax.broadcasted_iota(jnp.int32, (LINE * NB, BLK), 1)
    wanted = jnp.zeros((LINE * NB, BLK), jnp.int32)
    for k, mask in enumerate(MASKS):
        unit = row ^ (mask * (1 + (SIDE - 1) * odd))
        wanted = jnp.where(rows // NB == k, unit * NB + rows % NB, wanted)
    pick = jnp.where(wanted == lanes, 1.0, 0.0).astype(jnp.bfloat16)
    for k, source in enumerate(sources):
        extra = source[UNIT:ROWS, :BLK]
        count = dot_nt(pick, extra)
        level = jnp.where(count > 0.5, jnp.log2(jnp.maximum(count, 1.0)), -1e30)
        parts = extra.astype(jnp.float32)
        for b in range(NB):
            norm = parts[NB + b : NB + b + 1] + parts[2 * NB + b : 2 * NB + b + 1] + parts[3 * NB + b : 3 * NB + b + 1]
            bias[:, k * UNIT + b * BLK : k * UNIT + (b + 1) * BLK] = (
                level[:, b : b + 1] - norm * (2.0 * LOG2E / DIM)
            )


def near_sum(left, t, sources, bias, total=None):
    for k, source in enumerate(sources):
        cross = dot_nt(left, source[:UNIT, :DIM])
        tiles = []
        for b in range(NB):
            i = t * NB + b
            row = bias[i : i + 1, k * UNIT : (k + 1) * UNIT]
            tiles.append(
                jnp.exp2(cross[b * BLK : (b + 1) * BLK, :] * (4.0 * LOG2E / DIM) + row).astype(jnp.bfloat16)
            )
        tile = jnp.concatenate(tiles, axis=0)
        part = jnp.dot(tile, source[:UNIT, DIM:], preferred_element_type=jnp.float32)
        total = part if total is None else total + part
    return total


def near_first_kernel(s0, s1, s2, t1, own, total1, bias):
    sources = (s0, s1, s2)
    bias_rows(sources, bias)
    own[...] = near_sum(s0[:UNIT, :DIM], 0, sources, bias)
    total1[...] = near_sum(t1[...], 1, sources, bias)


def near_out_kernel(s0, s1, s2, s3, t1, t23, total1, bias, out, last):
    bias_rows((s3,), last)
    total3 = near_sum(t23[UNIT:, :], 3, (s0, s1, s2), bias)
    out[UNIT:, :] = near_sum(t23[UNIT:, :], 3, (s3,), last, total3).astype(jnp.bfloat16)
    out[:UNIT, :] = near_sum(t1[...], 1, (s3,), last, total1[...]).astype(jnp.bfloat16)


def near_in_kernel(s0, s1, s2, s3, t23, own, bias, last, own_out, out):
    total2 = near_sum(t23[:UNIT, :], 2, (s0, s1, s2), bias)
    out[...] = near_sum(t23[:UNIT, :], 2, (s3,), last, total2)
    own_out[...] = near_sum(s0[:UNIT, :DIM], 0, (s3,), last, own[...])


def relay_kernel(mine, received, out):
    out[...] = (mine[...] + received[UNIT:, :].astype(jnp.float32)).astype(jnp.bfloat16)


def finish_kernel(own, first, second, scale, out):
    total = own[...] + first[:UNIT, :].astype(jnp.float32) + second[...].astype(jnp.float32)
    out[...] = (total * scale[...]).astype(jnp.bfloat16)


def call(kernel, shapes, *args, micros=1.0, scratch=(), space=pltpu.VMEM, vmem=VMEM):
    return pl.pallas_call(
        kernel,
        out_shape=shapes,
        in_specs=[pl.BlockSpec(memory_space=space)] * len(args),
        out_specs=jax.tree.map(lambda _: pl.BlockSpec(memory_space=space), shapes),
        scratch_shapes=list(scratch),
        compiler_params=pltpu.CompilerParams(vmem_limit_bytes=vmem),
        cost_estimate=pl.CostEstimate(flops=int(micros * 1e9), bytes_accessed=int(micros * 3e6), transcendentals=0),
    )(*args)


def exchange(value, mask, first):
    n_col = lax.axis_size("col")
    pairs = []
    for y in range(SIDE):
        for x in range(SIDE):
            for c in range(n_col):
                along_x = c % 2 == first
                other = y * SIDE + (x ^ mask) if along_x else (y ^ mask) * SIDE + x
                pairs.append(((y * SIDE + x) * n_col + c, other * n_col + c))
    return lax.ppermute(value, ("row", "col"), pairs)


def partner(value, mask):
    return lax.ppermute(value, "col", [(c, c ^ mask) for c in range(lax.axis_size("col"))])


def on_device(points, weights, near_blocks, proxies):
    f32, bf16 = jnp.float32, jnp.bfloat16
    shape = jax.ShapeDtypeStruct
    t1 = exchange(points, 1, 0)
    send = call(
        send_kernel,
        shape((ROWS, DIM + NV), bf16),
        points,
        weights,
        near_blocks,
        scratch=[
            pltpu.VMEM((ROWS, DIM + NV), bf16),
            pltpu.VMEM(near_blocks.shape, jnp.int32),
            pltpu.SemaphoreType.DMA((6,)),
        ],
        space=pltpu.HBM,
        vmem=SEND_VMEM,
    )
    s1 = exchange(send, 3, 1)
    s2 = exchange(send, 1, 1)
    t23 = exchange(jnp.concatenate([points, t1], axis=0), 3, 0)
    proxies, t1 = lax.optimization_barrier((proxies, t1))
    gram, scale = call(gram_kernel, (shape((RANK, RANK), f32), shape((UNIT, NV), f32)), points, proxies)
    s3 = exchange(s1, 1, 1)
    unit = shape((UNIT, NV), f32)
    own, total1, bias = call(
        near_first_kernel, (unit, unit, shape((LINE * NB, 3 * UNIT), f32)), send, s1, s2, t1, micros=20.0
    )
    gram, total1 = lax.optimization_barrier((gram, total1))
    g1 = partner(gram, 1)
    g1, total1 = lax.optimization_barrier((g1, total1))
    g2 = partner(gram + g1, 2)
    sources = (send, s1, s2, s3)
    out, last = call(
        near_out_kernel,
        (shape((2 * UNIT, NV), bf16), shape((LINE * NB, UNIT), f32)),
        *sources,
        t1,
        t23,
        total1,
        bias,
    )
    r1 = exchange(out, 1, 0)
    own, mine = call(near_in_kernel, (unit, unit), *sources, t23, own, bias, last)
    relayed = call(relay_kernel, shape((UNIT, NV), bf16), mine, r1)
    r2 = exchange(relayed, 3, 0)
    gram, own = lax.optimization_barrier((gram, own))
    factors = call(factor_kernel, shape((RANK, 3 * RANK), f32), gram, g1, g2, micros=3.4)
    near_product = call(finish_kernel, shape((UNIT, NV), bf16), own, r1, r2, scale)
    return (near_product, factors)


def solution(mesh):
    placed = (P(("col", "row"), None), P(("col", "row"), None), P(("col", "row"), None), P())
    return jax.shard_map(
        on_device,
        mesh=mesh,
        in_specs=placed,
        out_specs=(P(("col", "row"), None), P(("col", "row"), None)),
        check_vma=False,
    )
```

```python
import functools

import jax
import jax.numpy as jnp
import numpy as np
from jax import lax
from jax.experimental import pallas as pl
from jax.experimental.pallas import tpu as pltpu
from jax.sharding import PartitionSpec as P

DIM = 256
RANK = 64
BLK = 128
NV = 128
UNIT = 512
NB = 4
SIDE = 4
EXTRA = 16
ROWS = UNIT + EXTRA
GROUP = 64
LOG2E = 1.4426950408889634
LINE = 4
MASKS = (0, 3, 1, 2)
PANEL = 4
NT = (((1,), (1,)), ((), ()))
HIGH = lax.Precision.HIGHEST
VMEM = 24 * 1024 * 1024
SEND_VMEM = 62 * 1024 * 1024


def dot_nt(a, b, precision=None):
    return lax.dot_general(a, b, NT, precision=precision, preferred_element_type=jnp.float32)


def split2(x):
    hi = x.astype(jnp.bfloat16)
    return hi, (x - hi.astype(jnp.float32)).astype(jnp.bfloat16)


def row_norms(squares):
    hi, lo = squares
    ones = jnp.ones((8, DIM), jnp.bfloat16)
    return dot_nt(ones, hi) + dot_nt(ones, lo)


def send_kernel(points, weights, near, send, held, ids, sems):
    unit, left, right = pl.ds(0, UNIT), pl.ds(0, DIM), pl.ds(DIM, NV)
    arriving = [
        pltpu.make_async_copy(points, held.at[unit, left], sems.at[0]),
        pltpu.make_async_copy(near, ids, sems.at[1]),
        pltpu.make_async_copy(weights, held.at[unit, right], sems.at[2]),
    ]
    leaving = [
        pltpu.make_async_copy(held.at[unit, left], send.at[unit, left], sems.at[3]),
        pltpu.make_async_copy(held.at[unit, right], send.at[unit, right], sems.at[4]),
        pltpu.make_async_copy(held.at[pl.ds(UNIT, EXTRA), :], send.at[pl.ds(UNIT, EXTRA), :], sems.at[5]),
    ]
    for copy in arriving:
        copy.start()
    held[UNIT:, BLK:] = jnp.zeros((EXTRA, DIM + NV - BLK), jnp.bfloat16)
    arriving[1].wait()
    local = ids[...] & (GROUP - 1)
    lanes = lax.broadcasted_iota(jnp.int32, (NB, BLK), 1)
    counts = jnp.zeros((NB, BLK), jnp.float32)
    for t in range(near.shape[1]):
        counts = counts + jnp.where(local[:, t : t + 1] == lanes, 1.0, 0.0)
    arriving[0].wait()
    leaving[0].start()
    arriving[2].wait()
    leaving[1].start()
    f = held[:UNIT, :DIM].astype(jnp.float32)
    norm = row_norms(split2(f * f))
    rows = jnp.concatenate([norm[0:1, b * BLK : (b + 1) * BLK] for b in range(NB)], axis=0)
    first = rows.astype(jnp.bfloat16).astype(jnp.float32)
    second = (rows - first).astype(jnp.bfloat16).astype(jnp.float32)
    third = rows - first - second
    extra = jnp.concatenate([counts, first, second, third], axis=0)
    held[UNIT:, :BLK] = extra.astype(jnp.bfloat16)
    leaving[2].start()
    for copy in leaving:
        copy.wait()


def gram_kernel(points, proxies, gram, scale):
    p = points[...]
    f = p.astype(jnp.float32)
    squares = split2(f * f)
    tall = jnp.ones((DIM, NV), jnp.bfloat16)
    column = jnp.dot(squares[0], tall, preferred_element_type=jnp.float32) + jnp.dot(
        squares[1], tall, preferred_element_type=jnp.float32
    )
    scale[...] = jnp.exp(column * (-2.0 / DIM))
    q = proxies[...]
    qf = q.astype(jnp.float32)
    qnorm = jnp.sum(qf * qf, axis=1, keepdims=True)
    far = jnp.exp((qnorm + row_norms(squares)[0:1, :] - 2.0 * dot_nt(q, p)) * (-2.0 / DIM))
    gram[...] = dot_nt(far, far, HIGH)


def factor_kernel(g0, s1, s2, out):
    zeros = jnp.zeros((RANK, RANK), jnp.float32)
    rows = lax.broadcasted_iota(jnp.int32, (RANK, 2 * RANK), 0)
    lanes = lax.broadcasted_iota(jnp.int32, (RANK, 2 * RANK), 1)
    eye = jnp.where(rows == lanes - RANK, 1.0, 0.0)
    gram0 = g0[...]
    gram1 = gram0 + s1[...]
    gram2 = gram1 + s2[...]
    work = []
    for g in (gram0, gram1, gram2):
        full = jnp.concatenate([g, zeros], axis=1) + eye
        work.append([full[8 * b : 8 * b + 8, :] for b in range(RANK // 8)])
    sub = lax.broadcasted_iota(jnp.int32, (8, 2 * RANK), 0)
    lane = lax.broadcasted_iota(jnp.int32, (8, 2 * RANK), 1)
    for k0 in range(0, RANK, PANEL):
        b0 = k0 // 8
        cols = [
            [
                {b: jnp.broadcast_to(w[b][:, k : k + 1], (8, 2 * RANK)) for b in range(b0, RANK // 8)}
                for k in range(k0, k0 + PANEL)
            ]
            for w in work
        ]
        for j in range(PANEL):
            s0 = (k0 + j) % 8
            for w, c in zip(work, cols):
                inverse = -1.0 / c[j][b0][s0 : s0 + 1, :]
                row = w[b0][s0 : s0 + 1, :] * inverse
                later = [c[i][b0][s0 : s0 + 1, :] * inverse for i in range(j + 1, PANEL)]
                for b in range(b0, RANK // 8):
                    col = c[j][b]
                    if b == b0:
                        if s0 == 7:
                            continue
                        col = jnp.where(sub > s0, col, 0.0)
                    w[b] = w[b] + col * row
                    for i, entry in enumerate(later, j + 1):
                        c[i][b] = c[i][b] + col * entry
    uppers, inverses = [], []
    for m in range(3):
        done = []
        for b in range(RANK // 8):
            w = work[m][b]
            diag = jnp.sum(jnp.where(lane == sub + 8 * b, w, 0.0), axis=1, keepdims=True)
            w = w * lax.rsqrt(diag)
            done.append(jnp.where((lane >= RANK) | (lane >= sub + 8 * b), w, 0.0))
        full = jnp.concatenate(done, axis=0)
        uppers.append(full[:, :RANK])
        inverses.append(full[:, RANK:])
    out[:, 0:RANK] = dot_nt(uppers[0], inverses[1], HIGH)
    out[:, RANK : 2 * RANK] = dot_nt(uppers[1], inverses[2], HIGH)
    out[:, 2 * RANK :] = uppers[2]


def bias_rows(sources, bias):
    row, odd = lax.axis_index("row"), lax.axis_index("col") & 1
    rows = lax.broadcasted_iota(jnp.int32, (LINE * NB, BLK), 0)
    lanes = lax.broadcasted_iota(jnp.int32, (LINE * NB, BLK), 1)
    wanted = jnp.zeros((LINE * NB, BLK), jnp.int32)
    for k, mask in enumerate(MASKS):
        unit = row ^ (mask * (1 + (SIDE - 1) * odd))
        wanted = jnp.where(rows // NB == k, unit * NB + rows % NB, wanted)
    pick = jnp.where(wanted == lanes, 1.0, 0.0).astype(jnp.bfloat16)
    for k, source in enumerate(sources):
        extra = source[UNIT:ROWS, :BLK]
        count = dot_nt(pick, extra)
        level = jnp.where(count > 0.5, jnp.log2(jnp.maximum(count, 1.0)), -1e30)
        parts = extra.astype(jnp.float32)
        for b in range(NB):
            norm = parts[NB + b : NB + b + 1] + parts[2 * NB + b : 2 * NB + b + 1] + parts[3 * NB + b : 3 * NB + b + 1]
            bias[:, k * UNIT + b * BLK : k * UNIT + (b + 1) * BLK] = (
                level[:, b : b + 1] - norm * (2.0 * LOG2E / DIM)
            )


def near_sum(left, t, sources, bias, total=None):
    for k, source in enumerate(sources):
        cross = dot_nt(left, source[:UNIT, :DIM])
        tiles = []
        for b in range(NB):
            i = t * NB + b
            row = bias[i : i + 1, k * UNIT : (k + 1) * UNIT]
            tiles.append(
                jnp.exp2(cross[b * BLK : (b + 1) * BLK, :] * (4.0 * LOG2E / DIM) + row).astype(jnp.bfloat16)
            )
        tile = jnp.concatenate(tiles, axis=0)
        part = jnp.dot(tile, source[:UNIT, DIM:], preferred_element_type=jnp.float32)
        total = part if total is None else total + part
    return total


def near_first_kernel(s0, s1, t1, t23, own, *rest):
    others, bias = rest[:-1], rest[-1]
    bias_rows((s0, s1), bias)
    own[...] = near_sum(s0[:UNIT, :DIM], 0, (s0, s1), bias)
    lefts = (t1, t23.at[pl.ds(0, UNIT)], t23.at[pl.ds(UNIT, UNIT)])
    for t, (left, other) in enumerate(zip(lefts, others), 1):
        other[...] = near_sum(left[...], t, (s0, s1), bias)


def near_out_kernel(s2, s3, t1, t23, total1, total3, out, bias):
    bias_rows((s2, s3), bias)
    out[UNIT:, :] = near_sum(t23[UNIT:, :], 3, (s2, s3), bias, total3[...]).astype(jnp.bfloat16)
    out[:UNIT, :] = near_sum(t1[...], 1, (s2, s3), bias, total1[...]).astype(jnp.bfloat16)


def near_in_kernel(s0, s2, s3, t23, own, total2, bias, own_out, out):
    out[...] = near_sum(t23[:UNIT, :], 2, (s2, s3), bias, total2[...])
    own_out[...] = near_sum(s0[:UNIT, :DIM], 0, (s2, s3), bias, own[...])


def relay_kernel(mine, received, out):
    out[...] = (mine[...] + received[UNIT:, :].astype(jnp.float32)).astype(jnp.bfloat16)


def finish_kernel(own, first, second, scale, out):
    total = own[...] + first[:UNIT, :].astype(jnp.float32) + second[...].astype(jnp.float32)
    out[...] = (total * scale[...]).astype(jnp.bfloat16)


def call(kernel, shapes, *args, micros=1.0, scratch=(), space=pltpu.VMEM, vmem=VMEM):
    return pl.pallas_call(
        kernel,
        out_shape=shapes,
        in_specs=[pl.BlockSpec(memory_space=space)] * len(args),
        out_specs=jax.tree.map(lambda _: pl.BlockSpec(memory_space=space), shapes),
        scratch_shapes=list(scratch),
        compiler_params=pltpu.CompilerParams(vmem_limit_bytes=vmem),
        cost_estimate=pl.CostEstimate(flops=int(micros * 1e9), bytes_accessed=int(micros * 3e6), transcendentals=0),
    )(*args)


def exchange(value, mask, first):
    n_col = lax.axis_size("col")
    pairs = []
    for y in range(SIDE):
        for x in range(SIDE):
            for c in range(n_col):
                along_x = c % 2 == first
                other = y * SIDE + (x ^ mask) if along_x else (y ^ mask) * SIDE + x
                pairs.append(((y * SIDE + x) * n_col + c, other * n_col + c))
    return lax.ppermute(value, ("row", "col"), pairs)


def partner(value, mask):
    return lax.ppermute(value, "col", [(c, c ^ mask) for c in range(lax.axis_size("col"))])


def on_device(points, weights, near_blocks, proxies):
    f32, bf16 = jnp.float32, jnp.bfloat16
    shape = jax.ShapeDtypeStruct
    t1 = exchange(points, 3, 0)
    send = call(
        send_kernel,
        shape((ROWS, DIM + NV), bf16),
        points,
        weights,
        near_blocks,
        scratch=[
            pltpu.VMEM((ROWS, DIM + NV), bf16),
            pltpu.VMEM(near_blocks.shape, jnp.int32),
            pltpu.SemaphoreType.DMA((6,)),
        ],
        space=pltpu.HBM,
        vmem=SEND_VMEM,
    )
    s1 = exchange(send, 3, 1)
    s2 = exchange(send, 1, 1)
    t23 = exchange(jnp.concatenate([points, t1], axis=0), 1, 0)
    proxies, t1 = lax.optimization_barrier((proxies, t1))
    gram, scale = call(gram_kernel, (shape((RANK, RANK), f32), shape((UNIT, NV), f32)), points, proxies)
    s3 = exchange(s1, 1, 1)
    gram, s1 = lax.optimization_barrier((gram, s1))
    g1 = partner(gram, 1)
    half = shape((LINE * NB, 2 * UNIT), f32)
    unit = shape((UNIT, NV), f32)
    own, total1, total2, total3 = call(
        near_first_kernel,
        (unit,) * LINE,
        send,
        s1,
        t1,
        t23,
        scratch=[pltpu.VMEM(half.shape, f32)],
    )
    g1, total1 = lax.optimization_barrier((g1, total1))
    g2 = partner(gram + g1, 2)
    out, bias23 = call(
        near_out_kernel, (shape((2 * UNIT, NV), bf16), half), s2, s3, t1, t23, total1, total3
    )
    r1 = exchange(out, 3, 0)
    own, mine = call(near_in_kernel, (unit, unit), send, s2, s3, t23, own, total2, bias23)
    relayed = call(relay_kernel, shape((UNIT, NV), bf16), mine, r1)
    r2 = exchange(relayed, 1, 0)
    gram, own = lax.optimization_barrier((gram, own))
    factors = call(factor_kernel, shape((RANK, 3 * RANK), f32), gram, g1, g2, micros=3.4)
    near_product = call(finish_kernel, shape((UNIT, NV), bf16), own, r1, r2, scale)
    return (near_product, factors)


def solution(mesh):
    placed = (P(("col", "row"), None), P(("col", "row"), None), P(("col", "row"), None), P())
    return jax.shard_map(
        on_device,
        mesh=mesh,
        in_specs=placed,
        out_specs=(P(("col", "row"), None), P(("col", "row"), None)),
        check_vma=False,
    )
```
